128 devices in a mesh: dp: 16 (over y, z), group: 8 (over x, core).
Axes of the slice: x: 4, y: 4, z: 4, core: 2. Of those that a mesh axis runs over, the one named last changes fastest.
Arguments:
- grad_partial: bfloat16 [16, 56, 1024, 1024], P('dp', 'group')
- left_root: bfloat16 [256, 1024, 1024], P(('dp', 'group'))
- right_root: bfloat16 [256, 1024, 1024], P(('dp', 'group'))
- block_owner: int32 [56], replicated, may hold values from 0 to 255, as said below
- momentum: float32 [56, 1024, 1024], P('group', 'dp'), may hold values from -6 to 6
Outputs:
- new_momentum: float32 [56, 1024, 1024], P('group', 'dp')
The draws below stay inside these ranges and needn't reach their ends.
Inputs may be any that keep to these rules, and one draw needn't show every extreme that they name: `block_owner`: distinct values. A value v names slot v % 2 of the device whose index over dp and group, dp slowest, is v // 2. Block b belongs to index b // 7 of group. The 7 blocks of each index of group go 4 to one owner group common to all indices and one each to 3 different other owner groups; no device holds two blocks of the same index of group; the common owner group holds 32 blocks.
All inputs are finite; a program needn't handle non-finite values.
Results may differ from the reference program's by a relative error of at most 0.018.
Values may be sent and summed in bfloat16 or wider, within the bound.
No kernel may reach another device: no remote copies, remote signals or barrier semaphores. Data moves between devices by JAX's collectives and lax.ppermute only.
A program may use at most 128 MiB of HBM per device.

```python
import math
import jax
import jax.numpy as jnp
from jax import lax

B = 1024
NBG = 7
CAPG = 4
SLOTD = 2
NB = 56
N_DP = 16
N_GROUP = 8


def factor_matrix(key, low_log, high_log):
    key_diag, key_off = jax.random.split(key)
    count = N_DP * N_GROUP * SLOTD
    diagonal = jnp.exp(jax.random.uniform(key_diag, (count, B), jnp.float32, low_log, high_log))
    raw = jax.random.normal(key_off, (count, B, B), jnp.float32) * (0.6 / math.sqrt(B))
    eye = jnp.eye(B, dtype=jnp.float32)
    return (raw * (1.0 - eye) + diagonal[:, :, None] * eye).astype(jnp.bfloat16)


def draw_left_root(key, part):
    key = jax.random.fold_in(key, 1)
    return factor_matrix(key, math.log(0.5), math.log(1.5))


def draw_right_root(key, part):
    key = jax.random.fold_in(key, 2)
    return factor_matrix(key, math.log(0.5), math.log(1.5))


def draw_grad_partial(key, part):
    key = jax.random.fold_in(key, 3)
    key_own = jax.random.fold_in(key, 1)
    blocks = NBG * N_GROUP
    own_part = jax.random.normal(key_own, (N_DP, blocks, B, B), jnp.float32)
    value = 0.25 * own_part
    return value.astype(jnp.bfloat16)


def draw_block_owner(key, part):
    key = jax.random.fold_in(key, 4)
    key_hot, key_pos, key_other, key_dev, key_flip = jax.random.split(key, 5)
    blocks = NBG * N_GROUP
    hottest = jax.random.randint(key_hot, (), 0, N_GROUP)
    positions = jax.vmap(lambda sub: jax.random.permutation(sub, NBG))(jax.random.split(key_pos, N_GROUP))
    others = jax.vmap(lambda sub: jax.random.permutation(sub, N_GROUP - 1))(jax.random.split(key_other, N_GROUP))
    others = others + (others >= hottest).astype(jnp.int32)
    later = jnp.clip(positions - CAPG, 0, N_GROUP - 2)
    chosen = jnp.take_along_axis(others, later, axis=1)
    owner_group = jnp.where(positions < CAPG, hottest, chosen).reshape(blocks)
    block_ids = jnp.arange(blocks, dtype=jnp.int32)
    earlier = (block_ids[None, :] < block_ids[:, None]) & (owner_group[None, :] == owner_group[:, None])
    ranking = jnp.sum(earlier.astype(jnp.int32), axis=1)
    device_perm = jax.vmap(lambda sub: jax.random.permutation(sub, N_DP))(jax.random.split(key_dev, N_GROUP))
    owner_dp = device_perm[owner_group, ranking % N_DP]
    flipped = jax.random.randint(key_flip, (N_GROUP, N_DP), 0, SLOTD)
    slot_index = (ranking // N_DP + flipped[owner_group, owner_dp]) % SLOTD
    return ((owner_dp * N_GROUP + owner_group) * SLOTD + slot_index).astype(jnp.int32)


def levels(rng, extent, shards, smallest, high):
    def one(dim, parts):
        heights = jax.random.uniform(jax.random.fold_in(jax.random.fold_in(rng, 6), dim), (parts,), jnp.float32, smallest / len(shards), high / len(shards))
        return jnp.repeat(jnp.exp(heights), extent[dim] // parts).reshape((-1,) + (1,) * (len(extent) - dim - 1))

    gain = one(*shards[0])
    for cut in shards[1:]:
        gain = gain * one(*cut)
    return gain


def bell_draw(stream_key, extent, scale, reach, cuts=(), kind=jnp.bfloat16):
    values = jax.random.normal(stream_key, extent, jnp.float32) * scale
    if len(cuts) > 0:
        values = levels(stream_key, extent, cuts, -0.22, 0.18) * values
    return jnp.clip(values, min=-reach, max=reach).astype(kind)


def setup_inputs(seed: int = 0) -> dict:
    splits = jax.random.split(jax.random.key(seed), 6)
    grad_partial = draw_grad_partial(jax.random.fold_in(splits[5], 71), 0)
    left_root = draw_left_root(jax.random.fold_in(splits[5], 71), 0)
    right_root = draw_right_root(jax.random.fold_in(splits[5], 71), 0)
    block_owner = draw_block_owner(jax.random.fold_in(splits[5], 71), 0)
    momentum = bell_draw(splits[4], (NB, B, B), 1.0, 6.0, ((0, 8), (1, 16)), jnp.float32)
    return dict(grad_partial=grad_partial, left_root=left_root, right_root=right_root, block_owner=block_owner, momentum=momentum)


def reference(grad_partial, left_root, right_root, block_owner, momentum):

    def add_part(step_index, running):
        return running + grad_partial[step_index].astype(jnp.float32)
    summed = lax.fori_loop(0, N_DP, add_part, jnp.zeros((NB, B, B), jnp.float32))
    gradient = summed.astype(jnp.bfloat16)

    def precondition(block_index):
        slot_index = block_owner[block_index]
        grad_block = gradient[block_index]
        left_part = jnp.dot(left_root[slot_index], grad_block, preferred_element_type=jnp.float32).astype(jnp.bfloat16)
        product = jnp.dot(left_part, right_root[slot_index], preferred_element_type=jnp.float32)
        grad_norm = jnp.sqrt(jnp.mean(jnp.square(grad_block.astype(jnp.float32))))
        prod_norm = jnp.sqrt(jnp.mean(product * product) + 1e-06)
        return (product * (grad_norm / prod_norm)).astype(jnp.bfloat16)
    direction = lax.map(precondition, jnp.arange(NB, dtype=jnp.int32))
    return 0.9 * momentum + direction.astype(jnp.float32)
```

```python
import functools

import jax
import jax.numpy as jnp
from jax import lax
from jax.experimental import pallas as pl
from jax.experimental.pallas import tpu as pltpu
from jax.sharding import PartitionSpec as P

CAPG = 4
CHUNKS = 2
STRIP = 256


def move_kernel(count, index_ref, source_ref, out_ref, sems):
    copies = [
        pltpu.make_async_copy(source_ref.at[index_ref[i]], out_ref.at[i], sems.at[i])
        for i in range(count)
    ]
    for copy in copies:
        copy.start()
    for copy in copies:
        copy.wait()


def move(source, index):
    count = index.shape[0]
    size = source.size // source.shape[0] * source.dtype.itemsize
    return pl.pallas_call(
        functools.partial(move_kernel, count),
        out_shape=jax.ShapeDtypeStruct((count,) + source.shape[1:], source.dtype),
        in_specs=[
            pl.BlockSpec(memory_space=pltpu.SMEM),
            pl.BlockSpec(memory_space=pl.ANY),
        ],
        out_specs=pl.BlockSpec(memory_space=pl.ANY),
        scratch_shapes=[pltpu.SemaphoreType.DMA((count,))],
        cost_estimate=pl.CostEstimate(
            flops=0, bytes_accessed=2 * count * size, transcendentals=0
        ),
        name="move",
    )(index, source)


def cut_kernel(chunk, source_ref, out_ref, sems):
    copies = [
        pltpu.make_async_copy(source_ref.at[:, d, chunk], out_ref.at[d], sems.at[d])
        for d in range(out_ref.shape[0])
    ]
    for copy in copies:
        copy.start()
    for copy in copies:
        copy.wait()


def cut(partial, chunk):
    blocks, places, _, rows, cols = partial.shape
    return pl.pallas_call(
        functools.partial(cut_kernel, chunk),
        out_shape=jax.ShapeDtypeStruct((places, blocks, rows, cols), partial.dtype),
        in_specs=[pl.BlockSpec(memory_space=pl.ANY)],
        out_specs=pl.BlockSpec(memory_space=pl.ANY),
        scratch_shapes=[pltpu.SemaphoreType.DMA((places,))],
        cost_estimate=pl.CostEstimate(
            flops=0, bytes_accessed=4 * places * blocks * rows * cols, transcendentals=0
        ),
        name="cut",
    )(partial)


def precondition_kernel(chunks, left_ref, right_ref, *refs):
    grads, outs = refs[:chunks], refs[chunks : 2 * chunks]
    block, product = refs[2 * chunks :]
    size = block.shape[0]
    for c in range(chunks):
        piece = grads[c].shape[2]
        for d in range(grads[c].shape[0]):
            start = (d * chunks + c) * piece
            block[start : start + piece, :] = grads[c][d, 0]
    grad_sum = jnp.zeros((1, size), jnp.float32)
    prod_sum = jnp.zeros((1, size), jnp.float32)
    for i in range(size // STRIP):
        rows = slice(i * STRIP, (i + 1) * STRIP)
        left_part = jnp.dot(
            left_ref[0, rows, :], block[...], preferred_element_type=jnp.float32
        ).astype(jnp.bfloat16)
        strip = jnp.dot(left_part, right_ref[0], preferred_element_type=jnp.float32)
        product[rows, :] = strip
        prod_sum += jnp.sum(strip * strip, axis=0, keepdims=True)
        grad = block[rows, :].astype(jnp.float32)
        grad_sum += jnp.sum(grad * grad, axis=0, keepdims=True)
    scale = 1.0 / (size * size)
    grad_norm = jnp.sqrt(jnp.sum(grad_sum, axis=1, keepdims=True) * scale)
    prod_norm = jnp.sqrt(jnp.sum(prod_sum, axis=1, keepdims=True) * scale + 1e-06)
    ratio = grad_norm / prod_norm
    for c in range(chunks):
        piece = outs[c].shape[2]
        for d in range(outs[c].shape[0]):
            start = (d * chunks + c) * piece
            outs[c][d, 0] = (product[start : start + piece, :] * ratio).astype(jnp.bfloat16)


def precondition(left_root, right_root, pieces):
    slots, size, _ = left_root.shape
    chunks = len(pieces)
    root_spec = pl.BlockSpec((1, size, size), lambda s: (s, 0, 0))
    part = pieces[0].shape
    part_spec = pl.BlockSpec((part[0], 1) + part[2:], lambda s: (0, s, 0, 0))
    return pl.pallas_call(
        functools.partial(precondition_kernel, chunks),
        grid=(slots,),
        out_shape=[jax.ShapeDtypeStruct(part, jnp.bfloat16)] * chunks,
        in_specs=[root_spec, root_spec] + [part_spec] * chunks,
        out_specs=[part_spec] * chunks,
        scratch_shapes=[
            pltpu.VMEM((size, size), jnp.bfloat16),
            pltpu.VMEM((size, size), jnp.float32),
        ],
        compiler_params=pltpu.CompilerParams(vmem_limit_bytes=48 * 1024 * 1024),
        cost_estimate=pl.CostEstimate(
            flops=4 * slots * size**3, bytes_accessed=8 * slots * size * size, transcendentals=0
        ),
        name="precondition",
    )(left_root, right_root, *pieces)


def update_kernel(chunks, index_ref, momentum_ref, *refs):
    parts, out = refs[:chunks], refs[chunks]
    for c in range(chunks):
        piece = parts[c].shape[1]
        rows = slice(c * piece, (c + 1) * piece)
        out[0, rows, :] = 0.9 * momentum_ref[0, rows, :] + parts[c][0].astype(jnp.float32)


def update(momentum, parts, index):
    chunks = len(parts)
    count, rows, cols = momentum.shape
    own = pl.BlockSpec((1, rows, cols), lambda j, index: (j, 0, 0))
    part = pl.BlockSpec((1, rows // chunks, cols), lambda j, index: (index[j], 0, 0))
    return pl.pallas_call(
        functools.partial(update_kernel, chunks),
        out_shape=jax.ShapeDtypeStruct(momentum.shape, jnp.float32),
        grid_spec=pltpu.PrefetchScalarGridSpec(
            num_scalar_prefetch=1,
            grid=(count,),
            in_specs=[own] + [part] * chunks,
            out_specs=own,
        ),
        name="update",
    )(index, momentum, *parts)


def pick(match, values):
    return jnp.sum(jnp.where(match, values[None, :], 0), axis=1).astype(jnp.int32)


def shards(grad_partial, left_root, right_root, block_owner, momentum):
    dp_count = lax.axis_size("dp")
    group_count = lax.axis_size("group")
    group_index = lax.axis_index("group")
    slot_count, size, _ = left_root.shape
    local_count, row_count, col_count = momentum.shape
    block_ids = jnp.arange(block_owner.shape[0], dtype=jnp.int32)
    owner_device = block_owner // slot_count
    owner_group = owner_device % group_count
    owner_place = owner_device // group_count * slot_count + block_owner % slot_count
    source_group = block_ids // local_count
    earlier = (
        (block_ids[None, :] < block_ids[:, None])
        & (source_group[None, :] == source_group[:, None])
        & (owner_group[None, :] == owner_group[:, None])
    )
    rank_in = jnp.sum(earlier.astype(jnp.int32), axis=1)
    buffer_size = group_count * CAPG
    column = source_group * CAPG + rank_in
    target = lax.dynamic_slice_in_dim(
        owner_group * CAPG + rank_in, group_index * local_count, local_count
    )
    held_here = (owner_group == group_index)[None, :]
    columns = jnp.arange(buffer_size, dtype=jnp.int32)[:, None]
    places = jnp.arange(dp_count * slot_count, dtype=jnp.int32)[:, None]
    to_group = pick(target[None, :] == columns, jnp.arange(local_count, dtype=jnp.int32))
    to_owner = pick(held_here & (owner_place[None, :] == places), column)
    to_source = pick(held_here & (column[None, :] == columns), owner_place)

    piece = row_count // CHUNKS
    partial = grad_partial[0].reshape(local_count, dp_count, CHUNKS, piece, col_count)
    pieces = []
    for c in range(CHUNKS):
        rows = lax.psum_scatter(cut(partial, c), "dp", scatter_dimension=0, tiled=True)
        sent = move(rows.reshape(local_count, piece, col_count), to_group)
        sent = sent.reshape(group_count, CAPG * piece, col_count)
        came = lax.all_to_all(sent, "group", split_axis=0, concat_axis=0, tiled=True)
        sent = move(came.reshape(buffer_size, piece, col_count), to_owner)
        sent = sent.reshape(dp_count, slot_count * piece, col_count)
        came = lax.all_to_all(sent, "dp", split_axis=0, concat_axis=0, tiled=True)
        pieces.append(came.reshape(dp_count, slot_count, piece, col_count))
    directions = precondition(left_root, right_root, pieces)
    parts = []
    for c in range(CHUNKS):
        sent = directions[c].reshape(dp_count, slot_count * piece, col_count)
        came = lax.all_to_all(sent, "dp", split_axis=0, concat_axis=0, tiled=True)
        sent = move(came.reshape(dp_count * slot_count, piece, col_count), to_source)
        sent = sent.reshape(group_count, CAPG * piece, col_count)
        came = lax.all_to_all(sent, "group", split_axis=0, concat_axis=0, tiled=True)
        parts.append(came.reshape(buffer_size, piece, col_count))
    return update(momentum, parts, target)


def solution(mesh):
    return jax.shard_map(
        shards,
        mesh=mesh,
        in_specs=(
            P("dp", "group", None, None),
            P(("dp", "group"), None, None),
            P(("dp", "group"), None, None),
            P(),
            P("group", "dp", None),
        ),
        out_specs=P("group", "dp", None),
        check_vma=False,
    )
```

```python
import functools

import jax
import jax.numpy as jnp
from jax import lax
from jax.experimental import pallas as pl
from jax.experimental.pallas import tpu as pltpu
from jax.sharding import PartitionSpec as P

CAPG = 4
CHUNKS = 2
STRIP = 256
VMEM_LIMIT = 48 * 1024 * 1024


def stage(sources, targets, buffer, loads, stores):
    count = len(sources)
    first = [
        pltpu.make_async_copy(sources[i], buffer.at[i], loads.at[i]) for i in range(count)
    ]
    second = [
        pltpu.make_async_copy(buffer.at[i], targets[i], stores.at[i]) for i in range(count)
    ]
    for copy in first:
        copy.start()
    for i in range(count):
        first[i].wait()
        second[i].start()
    for copy in second:
        copy.wait()


def staging(count, shape, dtype):
    return [
        pltpu.VMEM((count,) + shape, dtype),
        pltpu.SemaphoreType.DMA((count,)),
        pltpu.SemaphoreType.DMA((count,)),
    ]


def move_kernel(count, index_ref, source_ref, out_ref, buffer, loads, stores):
    stage(
        [source_ref.at[index_ref[i]] for i in range(count)],
        [out_ref.at[i] for i in range(count)],
        buffer,
        loads,
        stores,
    )


def move(source, index):
    count = index.shape[0]
    size = source.size // source.shape[0] * source.dtype.itemsize
    return pl.pallas_call(
        functools.partial(move_kernel, count),
        out_shape=jax.ShapeDtypeStruct((count,) + source.shape[1:], source.dtype),
        in_specs=[
            pl.BlockSpec(memory_space=pltpu.SMEM),
            pl.BlockSpec(memory_space=pl.ANY),
        ],
        out_specs=pl.BlockSpec(memory_space=pl.ANY),
        scratch_shapes=staging(count, source.shape[1:], source.dtype),
        compiler_params=pltpu.CompilerParams(vmem_limit_bytes=VMEM_LIMIT),
        cost_estimate=pl.CostEstimate(
            flops=0, bytes_accessed=2 * count * size, transcendentals=0
        ),
        name="move",
    )(index, source)


def cut_kernel(chunk, source_ref, out_ref, buffer, loads, stores):
    places = out_ref.shape[0]
    stage(
        [source_ref.at[:, d, chunk] for d in range(places)],
        [out_ref.at[d] for d in range(places)],
        buffer,
        loads,
        stores,
    )


def cut(partial, chunk):
    blocks, places, _, rows, cols = partial.shape
    return pl.pallas_call(
        functools.partial(cut_kernel, chunk),
        out_shape=jax.ShapeDtypeStruct((places, blocks, rows, cols), partial.dtype),
        in_specs=[pl.BlockSpec(memory_space=pl.ANY)],
        out_specs=pl.BlockSpec(memory_space=pl.ANY),
        scratch_shapes=staging(places, (blocks, rows, cols), partial.dtype),
        compiler_params=pltpu.CompilerParams(vmem_limit_bytes=VMEM_LIMIT),
        cost_estimate=pl.CostEstimate(
            flops=0, bytes_accessed=4 * places * blocks * rows * cols, transcendentals=0
        ),
        name="cut",
    )(partial)


def precondition_kernel(chunks, left_ref, right_ref, *refs):
    grads, outs = refs[:chunks], refs[chunks : 2 * chunks]
    block, product = refs[2 * chunks :]
    size = block.shape[0]
    for c in range(chunks):
        piece = grads[c].shape[2]
        for d in range(grads[c].shape[0]):
            start = (d * chunks + c) * piece
            block[start : start + piece, :] = grads[c][d, 0]
    grad_sum = jnp.zeros((1, size), jnp.float32)
    prod_sum = jnp.zeros((1, size), jnp.float32)
    for i in range(size // STRIP):
        rows = slice(i * STRIP, (i + 1) * STRIP)
        left_part = jnp.dot(
            left_ref[0, rows, :], block[...], preferred_element_type=jnp.float32
        ).astype(jnp.bfloat16)
        strip = jnp.dot(left_part, right_ref[0], preferred_element_type=jnp.float32)
        product[rows, :] = strip
        prod_sum += jnp.sum(strip * strip, axis=0, keepdims=True)
        grad = block[rows, :].astype(jnp.float32)
        grad_sum += jnp.sum(grad * grad, axis=0, keepdims=True)
    scale = 1.0 / (size * size)
    grad_norm = jnp.sqrt(jnp.sum(grad_sum, axis=1, keepdims=True) * scale)
    prod_norm = jnp.sqrt(jnp.sum(prod_sum, axis=1, keepdims=True) * scale + 1e-06)
    ratio = grad_norm / prod_norm
    for c in range(chunks):
        piece = outs[c].shape[2]
        for d in range(outs[c].shape[0]):
            start = (d * chunks + c) * piece
            outs[c][d, 0] = (product[start : start + piece, :] * ratio).astype(jnp.bfloat16)


def precondition(left_root, right_root, pieces):
    slots, size, _ = left_root.shape
    chunks = len(pieces)
    root_spec = pl.BlockSpec((1, size, size), lambda s: (s, 0, 0))
    part = pieces[0].shape
    part_spec = pl.BlockSpec((part[0], 1) + part[2:], lambda s: (0, s, 0, 0))
    return pl.pallas_call(
        functools.partial(precondition_kernel, chunks),
        grid=(slots,),
        out_shape=[jax.ShapeDtypeStruct(part, jnp.bfloat16)] * chunks,
        in_specs=[root_spec, root_spec] + [part_spec] * chunks,
        out_specs=[part_spec] * chunks,
        scratch_shapes=[
            pltpu.VMEM((size, size), jnp.bfloat16),
            pltpu.VMEM((size, size), jnp.float32),
        ],
        compiler_params=pltpu.CompilerParams(vmem_limit_bytes=VMEM_LIMIT),
        cost_estimate=pl.CostEstimate(
            flops=4 * slots * size**3, bytes_accessed=8 * slots * size * size, transcendentals=0
        ),
        name="precondition",
    )(left_root, right_root, *pieces)


def update_kernel(chunks, index_ref, momentum_ref, *refs):
    parts, out = refs[:chunks], refs[chunks]
    for c in range(chunks):
        piece = parts[c].shape[1]
        rows = slice(c * piece, (c + 1) * piece)
        out[0, rows, :] = 0.9 * momentum_ref[0, rows, :] + parts[c][0].astype(jnp.float32)


def update(momentum, parts, index):
    chunks = len(parts)
    count, rows, cols = momentum.shape
    own = pl.BlockSpec((1, rows, cols), lambda j, index: (j, 0, 0))
    part = pl.BlockSpec((1, rows // chunks, cols), lambda j, index: (index[j], 0, 0))
    return pl.pallas_call(
        functools.partial(update_kernel, chunks),
        out_shape=jax.ShapeDtypeStruct(momentum.shape, jnp.float32),
        grid_spec=pltpu.PrefetchScalarGridSpec(
            num_scalar_prefetch=1,
            grid=(count,),
            in_specs=[own] + [part] * chunks,
            out_specs=own,
        ),
        name="update",
    )(index, momentum, *parts)


def pick(match, values):
    return jnp.sum(jnp.where(match, values[None, :], 0), axis=1).astype(jnp.int32)


def shards(grad_partial, left_root, right_root, block_owner, momentum):
    dp_count = lax.axis_size("dp")
    group_count = lax.axis_size("group")
    group_index = lax.axis_index("group")
    slot_count, size, _ = left_root.shape
    local_count, row_count, col_count = momentum.shape
    block_ids = jnp.arange(block_owner.shape[0], dtype=jnp.int32)
    owner_device = block_owner // slot_count
    owner_group = owner_device % group_count
    owner_place = owner_device // group_count * slot_count + block_owner % slot_count
    source_group = block_ids // local_count
    earlier = (
        (block_ids[None, :] < block_ids[:, None])
        & (source_group[None, :] == source_group[:, None])
        & (owner_group[None, :] == owner_group[:, None])
    )
    rank_in = jnp.sum(earlier.astype(jnp.int32), axis=1)
    buffer_size = group_count * CAPG
    column = source_group * CAPG + rank_in
    target = lax.dynamic_slice_in_dim(
        owner_group * CAPG + rank_in, group_index * local_count, local_count
    )
    held_here = (owner_group == group_index)[None, :]
    columns = jnp.arange(buffer_size, dtype=jnp.int32)[:, None]
    places = jnp.arange(dp_count * slot_count, dtype=jnp.int32)[:, None]
    to_group = pick(target[None, :] == columns, jnp.arange(local_count, dtype=jnp.int32))
    to_owner = pick(held_here & (owner_place[None, :] == places), column)
    to_source = pick(held_here & (column[None, :] == columns), owner_place)

    piece = row_count // CHUNKS
    partial = grad_partial[0].reshape(local_count, dp_count, CHUNKS, piece, col_count)
    pieces = []
    for c in range(CHUNKS):
        rows = lax.psum_scatter(cut(partial, c), "dp", scatter_dimension=0, tiled=True)
        sent = move(rows.reshape(local_count, piece, col_count), to_group)
        sent = sent.reshape(group_count, CAPG * piece, col_count)
        came = lax.all_to_all(sent, "group", split_axis=0, concat_axis=0, tiled=True)
        sent = move(came.reshape(buffer_size, piece, col_count), to_owner)
        sent = sent.reshape(dp_count, slot_count * piece, col_count)
        came = lax.all_to_all(sent, "dp", split_axis=0, concat_axis=0, tiled=True)
        pieces.append(came.reshape(dp_count, slot_count, piece, col_count))
    directions = precondition(left_root, right_root, pieces)
    parts = []
    for c in range(CHUNKS):
        sent = directions[c].reshape(dp_count, slot_count * piece, col_count)
        came = lax.all_to_all(sent, "dp", split_axis=0, concat_axis=0, tiled=True)
        sent = move(came.reshape(dp_count * slot_count, piece, col_count), to_source)
        sent = sent.reshape(group_count, CAPG * piece, col_count)
        came = lax.all_to_all(sent, "group", split_axis=0, concat_axis=0, tiled=True)
        parts.append(came.reshape(buffer_size, piece, col_count))
    return update(momentum, parts, target)


def solution(mesh):
    return jax.shard_map(
        shards,
        mesh=mesh,
        in_specs=(
            P("dp", "group", None, None),
            P(("dp", "group"), None, None),
            P(("dp", "group"), None, None),
            P(),
            P("group", "dp", None),
        ),
        out_specs=P("group", "dp", None),
        check_vma=False,
    )
```

```python
import functools

import jax
import jax.numpy as jnp
from jax import lax
from jax.experimental import pallas as pl
from jax.experimental.pallas import tpu as pltpu
from jax.sharding import PartitionSpec as P

CAPG = 4
STRIP = 256
VMEM_LIMIT = 48 * 1024 * 1024


def stage(valid, sources, targets, buffer, loads, stores):
    count = len(sources)

    def load(i):
        return pltpu.make_async_copy(sources[i], buffer.at[i], loads.at[i])

    def store(i):
        return pltpu.make_async_copy(buffer.at[i], targets[i], stores.at[i])

    for i in range(count):

        @pl.when(valid[i])
        def _(i=i):
            load(i).start()

    for i in range(count):

        @pl.when(valid[i])
        def _(i=i):
            load(i).wait()
            store(i).start()

    for i in range(count):

        @pl.when(valid[i])
        def _(i=i):
            store(i).wait()


def at_least_zero(index):
    return jnp.maximum(index, 0)


def spread_kernel(outs_shape, index_ref, source_ref, *refs):
    outs = refs[: len(outs_shape)]
    buffer, loads, stores = refs[len(outs_shape) :]
    targets = [out.at[i] for out in outs for i in range(out.shape[0])]
    count = len(targets)
    index = [index_ref[i] for i in range(count)]
    stage(
        [index[i] >= 0 for i in range(count)],
        [source_ref.at[at_least_zero(index[i])] for i in range(count)],
        targets,
        buffer,
        loads,
        stores,
    )


def staging(count, shape, dtype):
    return [
        pltpu.VMEM((count,) + shape, dtype),
        pltpu.SemaphoreType.DMA((count,)),
        pltpu.SemaphoreType.DMA((count,)),
    ]


def spread(source, index, sizes):
    count = sum(sizes)
    piece = source.shape[1:]
    bytes_moved = 2 * count * piece[0] * piece[1] * source.dtype.itemsize
    any_space = pl.BlockSpec(memory_space=pl.ANY)
    return pl.pallas_call(
        functools.partial(spread_kernel, sizes),
        out_shape=[jax.ShapeDtypeStruct((n,) + piece, source.dtype) for n in sizes],
        in_specs=[pl.BlockSpec(memory_space=pltpu.SMEM), any_space],
        out_specs=[any_space] * len(sizes),
        scratch_shapes=staging(count, piece, source.dtype),
        compiler_params=pltpu.CompilerParams(vmem_limit_bytes=VMEM_LIMIT),
        cost_estimate=pl.CostEstimate(flops=0, bytes_accessed=bytes_moved, transcendentals=0),
        name="spread",
    )(index, source)


def collect_kernel(parts, from_ref, to_ref, own_ref, *refs):
    sources = refs[:parts]
    out, buffer, loads, stores = refs[parts:]
    own = from_ref.shape[0]
    pieces = [own_ref.at[at_least_zero(from_ref[i])] for i in range(own)]
    pieces += [ref.at[i] for ref in sources for i in range(ref.shape[0])]
    index = [to_ref[i] for i in range(len(pieces))]
    stage(
        [i >= 0 for i in index],
        pieces,
        [out.at[at_least_zero(i)] for i in index],
        buffer,
        loads,
        stores,
    )


def collect(own, own_from, sources, to, count):
    piece = own.shape[1:]
    total = to.shape[0]
    any_space = pl.BlockSpec(memory_space=pl.ANY)
    bytes_moved = 2 * count * piece[0] * piece[1] * own.dtype.itemsize
    return pl.pallas_call(
        functools.partial(collect_kernel, len(sources)),
        out_shape=jax.ShapeDtypeStruct((count,) + piece, own.dtype),
        in_specs=[pl.BlockSpec(memory_space=pltpu.SMEM)] * 2 + [any_space] * (1 + len(sources)),
        out_specs=any_space,
        scratch_shapes=staging(total, piece, own.dtype),
        compiler_params=pltpu.CompilerParams(vmem_limit_bytes=VMEM_LIMIT),
        cost_estimate=pl.CostEstimate(flops=0, bytes_accessed=bytes_moved, transcendentals=0),
        name="collect",
    )(own_from, to, own, *sources)


def precondition_kernel(left_ref, right_ref, grad_ref, out_ref, block, product):
    size = block.shape[0]
    places, _, piece, _ = grad_ref.shape
    for d in range(places):
        block[d * piece : (d + 1) * piece, :] = grad_ref[d, 0]
    grad_sum = jnp.zeros((1, size), jnp.float32)
    prod_sum = jnp.zeros((1, size), jnp.float32)
    for i in range(size // STRIP):
        rows = slice(i * STRIP, (i + 1) * STRIP)
        left_part = jnp.dot(
            left_ref[0, rows, :], block[...], preferred_element_type=jnp.float32
        ).astype(jnp.bfloat16)
        strip = jnp.dot(left_part, right_ref[0], preferred_element_type=jnp.float32)
        product[rows, :] = strip
        prod_sum += jnp.sum(strip * strip, axis=0, keepdims=True)
        grad = block[rows, :].astype(jnp.float32)
        grad_sum += jnp.sum(grad * grad, axis=0, keepdims=True)
    scale = 1.0 / (size * size)
    grad_norm = jnp.sqrt(jnp.sum(grad_sum, axis=1, keepdims=True) * scale)
    prod_norm = jnp.sqrt(jnp.sum(prod_sum, axis=1, keepdims=True) * scale + 1e-06)
    ratio = grad_norm / prod_norm
    for d in range(places):
        rows = slice(d * piece, (d + 1) * piece)
        out_ref[d, 0] = (product[rows, :] * ratio).astype(jnp.bfloat16)


def precondition(left_root, right_root, pieces):
    slots, size, _ = left_root.shape
    root_spec = pl.BlockSpec((1, size, size), lambda s: (s, 0, 0))
    part = pieces.shape
    part_spec = pl.BlockSpec((part[0], 1) + part[2:], lambda s: (0, s, 0, 0))
    return pl.pallas_call(
        precondition_kernel,
        grid=(slots,),
        out_shape=jax.ShapeDtypeStruct(part, jnp.bfloat16),
        in_specs=[root_spec, root_spec, part_spec],
        out_specs=part_spec,
        scratch_shapes=[
            pltpu.VMEM((size, size), jnp.bfloat16),
            pltpu.VMEM((size, size), jnp.float32),
        ],
        compiler_params=pltpu.CompilerParams(vmem_limit_bytes=VMEM_LIMIT),
        cost_estimate=pl.CostEstimate(
            flops=4 * slots * size**3, bytes_accessed=8 * slots * size * size, transcendentals=0
        ),
        name="precondition",
    )(left_root, right_root, pieces)


def update_kernel(parts, from_ref, to_ref, momentum_ref, own_ref, *refs):
    sources = refs[:parts]
    out, buffer, loads = refs[parts:]
    own = from_ref.shape[0]
    pieces = [own_ref.at[at_least_zero(from_ref[i])] for i in range(own)]
    pieces += [ref.at[i] for ref in sources for i in range(ref.shape[0])]
    index = [to_ref[i] for i in range(len(pieces))]

    def load(i):
        return pltpu.make_async_copy(pieces[i], buffer.at[at_least_zero(index[i])], loads.at[i])

    for i in range(len(pieces)):

        @pl.when(index[i] >= 0)
        def _(i=i):
            load(i).start()

    for i in range(len(pieces)):

        @pl.when(index[i] >= 0)
        def _(i=i):
            load(i).wait()

    for j in range(buffer.shape[0]):
        out[j] = 0.9 * momentum_ref[j] + buffer[j].astype(jnp.float32)


def update(momentum, own, own_from, sources, to):
    any_space = pl.BlockSpec(memory_space=pl.ANY)
    return pl.pallas_call(
        functools.partial(update_kernel, len(sources)),
        out_shape=jax.ShapeDtypeStruct(momentum.shape, jnp.float32),
        in_specs=[pl.BlockSpec(memory_space=pltpu.SMEM)] * 2
        + [pl.BlockSpec(memory_space=pltpu.VMEM)]
        + [any_space] * (1 + len(sources)),
        out_specs=pl.BlockSpec(memory_space=pltpu.VMEM),
        scratch_shapes=[
            pltpu.VMEM(momentum.shape, own.dtype),
            pltpu.SemaphoreType.DMA((to.shape[0],)),
        ],
        compiler_params=pltpu.CompilerParams(vmem_limit_bytes=VMEM_LIMIT),
        name="update",
    )(own_from, to, momentum, own, *sources)


def table(match, values):
    return jnp.sum(jnp.where(match, values + 1, 0), axis=-1).astype(jnp.int32) - 1


def exchange(pieces, groups):
    shape = pieces.shape
    pieces = pieces.reshape(groups, -1, shape[-1])
    pieces = lax.all_to_all(pieces, "group", split_axis=0, concat_axis=0, tiled=True)
    return pieces.reshape(shape)


def to_owner_group(hot, groups, places, tables, rows):
    mine, place, group_index = tables
    others = [g for g in range(groups) if g != hot]
    ids = jnp.arange(groups, dtype=jnp.int32)
    single = (ids != hot) & (ids != group_index)
    send = jnp.concatenate([mine[hot], jnp.where(single, mine[:, 0], -1)])
    heavy, light = spread(rows, send, [CAPG, groups])
    came_heavy = [lax.ppermute(heavy, "group", [(g, hot)]) for g in others]
    came_light = exchange(light, groups)
    own_to = lax.dynamic_index_in_dim(place, group_index, keepdims=False)
    own_from = lax.dynamic_index_in_dim(mine, group_index, keepdims=False)
    here = group_index == hot
    heavy_to = [jnp.where(here, place[g], -1) for g in others]
    light_to = jnp.where((ids != group_index) & ~here, place[:, 0], -1)
    to = jnp.concatenate([own_to] + heavy_to + [light_to])
    return collect(rows, own_from, came_heavy + [came_light], to, places)


def to_momentum(hot, groups, tables, returned, momentum):
    mine, place, group_index = tables
    others = [g for g in range(groups) if g != hot]
    ids = jnp.arange(groups, dtype=jnp.int32)
    here = group_index == hot
    heavy_send = [jnp.where(here, place[g], -1) for g in others]
    light_send = jnp.where((ids != group_index) & ~here, place[:, 0], -1)
    send = jnp.concatenate(heavy_send + [light_send])
    sent = spread(returned, send, [CAPG] * len(others) + [groups])
    came_heavy = [
        lax.ppermute(sent[i], "group", [(hot, g)]) for i, g in enumerate(others)
    ]
    came_light = exchange(sent[-1], groups)
    own_from = lax.dynamic_index_in_dim(place, group_index, keepdims=False)
    own_to = lax.dynamic_index_in_dim(mine, group_index, keepdims=False)
    heavy_to = [jnp.where(group_index == g, mine[hot], -1) for g in others]
    light_to = jnp.where((ids != group_index) & (ids != hot), mine[:, 0], -1)
    to = jnp.concatenate([own_to] + heavy_to + [light_to])
    return update(momentum, returned, own_from, came_heavy + [came_light], to)


def shards(grad_partial, left_root, right_root, block_owner, momentum):
    dp_count = lax.axis_size("dp")
    groups = lax.axis_size("group")
    group_index = lax.axis_index("group")
    slot_count = left_root.shape[0]
    local_count, row_count, col_count = momentum.shape
    block_total = block_owner.shape[0]
    rows = lax.psum_scatter(grad_partial, "dp", scatter_dimension=2, tiled=True)[0]

    block_ids = jnp.arange(block_total, dtype=jnp.int32)
    owner_device = block_owner // slot_count
    owner_group = owner_device % groups
    owner_place = owner_device // groups * slot_count + block_owner % slot_count
    source_group = block_ids // local_count
    earlier = (
        (block_ids[None, :] < block_ids[:, None])
        & (source_group[None, :] == source_group[:, None])
        & (owner_group[None, :] == owner_group[:, None])
    )
    rank_in = jnp.sum(earlier.astype(jnp.int32), axis=1)
    ids = jnp.arange(groups, dtype=jnp.int32)
    ranks = jnp.arange(CAPG, dtype=jnp.int32)
    held = jnp.sum((owner_group[None, :] == ids[:, None]).astype(jnp.int32), axis=1)
    hot = jnp.argmax(held).astype(jnp.int32)
    ranked = rank_in[None, None, :] == ranks[None, :, None]
    mine = table(
        (source_group[None, None, :] == group_index)
        & (owner_group[None, None, :] == ids[:, None, None])
        & ranked,
        block_ids - group_index * local_count,
    )
    place = table(
        (source_group[None, None, :] == ids[:, None, None])
        & (owner_group[None, None, :] == group_index)
        & ranked,
        owner_place,
    )
    tables = (mine, place, group_index)

    places = dp_count * slot_count
    sent = lax.switch(
        hot,
        [functools.partial(to_owner_group, g, groups, places) for g in range(groups)],
        tables,
        rows,
    )
    sent = sent.reshape(dp_count, slot_count * row_count, col_count)
    came = lax.all_to_all(sent, "dp", split_axis=0, concat_axis=0, tiled=True)
    directions = precondition(
        left_root, right_root, came.reshape(dp_count, slot_count, row_count, col_count)
    )
    sent = directions.reshape(dp_count, slot_count * row_count, col_count)
    came = lax.all_to_all(sent, "dp", split_axis=0, concat_axis=0, tiled=True)
    return lax.switch(
        hot,
        [functools.partial(to_momentum, g, groups) for g in range(groups)],
        tables,
        came.reshape(places, row_count, col_count),
        momentum,
    )


def solution(mesh):
    return jax.shard_map(
        shards,
        mesh=mesh,
        in_specs=(
            P("dp", "group", None, None),
            P(("dp", "group"), None, None),
            P(("dp", "group"), None, None),
            P(),
            P("group", "dp", None),
        ),
        out_specs=P("group", "dp", None),
        check_vma=False,
    )
```

```python
import functools

import jax
import jax.numpy as jnp
from jax import lax
from jax.experimental import pallas as pl
from jax.experimental.pallas import tpu as pltpu
from jax.sharding import PartitionSpec as P

CAP = 5
CHUNKS = 1
STRIP = 256
VMEM_LIMIT = 48 * 1024 * 1024


def stage(copies, buffer, loads, stores):
    def load(i):
        return pltpu.make_async_copy(copies[i][1], buffer.at[i], loads.at[i])

    def store(i):
        return pltpu.make_async_copy(buffer.at[i], copies[i][2], stores.at[i])

    for i, (valid, _, _) in enumerate(copies):

        @pl.when(valid)
        def _(i=i):
            load(i).start()

    for i, (valid, _, _) in enumerate(copies):

        @pl.when(valid)
        def _(i=i):
            load(i).wait()
            store(i).start()

    for i, (valid, _, _) in enumerate(copies):

        @pl.when(valid)
        def _(i=i):
            store(i).wait()


def at_least_zero(index):
    return jnp.maximum(index, 0)


def staging(count, shape, dtype):
    return [
        pltpu.VMEM((count,) + shape, dtype),
        pltpu.SemaphoreType.DMA((count,)),
        pltpu.SemaphoreType.DMA((count,)),
    ]


def choose(index, refs, start, rows):
    found, first = [], 0
    for ref in refs:
        count = ref.shape[0]
        here = (index >= first) & (index < first + count)
        piece = jnp.clip(index - first, 0, count - 1)
        found.append((here, ref.at[piece, pl.ds(start, rows)]))
        first += count
    return found


def spread_kernel(parts, sizes, start, index_ref, *refs):
    sources, outs = refs[:parts], refs[parts : parts + len(sizes)]
    targets = [out.at[i] for out in outs for i in range(out.shape[0])]
    copies = []
    for i, target in enumerate(targets):
        for valid, piece in choose(index_ref[i], sources, start, outs[0].shape[1]):
            copies.append((valid, piece, target))
    stage(copies, *refs[parts + len(sizes) :])


def spread(sources, index, sizes, start, rows):
    count, piece = sum(sizes), (rows, sources[0].shape[2])
    dtype = sources[0].dtype
    any_space = pl.BlockSpec(memory_space=pl.ANY)
    return pl.pallas_call(
        functools.partial(spread_kernel, len(sources), sizes, start),
        out_shape=[jax.ShapeDtypeStruct((n,) + piece, dtype) for n in sizes],
        in_specs=[pl.BlockSpec(memory_space=pltpu.SMEM)] + [any_space] * len(sources),
        out_specs=[any_space] * len(sizes),
        scratch_shapes=staging(count * len(sources), piece, dtype),
        compiler_params=pltpu.CompilerParams(vmem_limit_bytes=VMEM_LIMIT),
        cost_estimate=pl.CostEstimate(
            flops=0, bytes_accessed=4 * count * piece[0] * piece[1], transcendentals=0
        ),
        name="spread",
    )(index, *sources)


def collect_kernel(parts, start, to_ref, *refs):
    sources, out = refs[:parts], refs[parts]
    rows = out.shape[1]
    pieces = []
    for ref in sources:
        first = start if ref.shape[1] > rows else 0
        pieces += [ref.at[i, pl.ds(first, rows)] for i in range(ref.shape[0])]
    copies = []
    for i, piece in enumerate(pieces):
        to = to_ref[i]
        copies.append((to >= 0, piece, out.at[at_least_zero(to)]))
    stage(copies, *refs[parts + 1 :])


def collect(sources, start, rows, to, count):
    piece = (rows, sources[0].shape[2])
    dtype = sources[0].dtype
    any_space = pl.BlockSpec(memory_space=pl.ANY)
    return pl.pallas_call(
        functools.partial(collect_kernel, len(sources), start),
        out_shape=jax.ShapeDtypeStruct((count,) + piece, dtype),
        in_specs=[pl.BlockSpec(memory_space=pltpu.SMEM)] + [any_space] * len(sources),
        out_specs=any_space,
        scratch_shapes=staging(to.shape[0], piece, dtype),
        compiler_params=pltpu.CompilerParams(vmem_limit_bytes=VMEM_LIMIT),
        cost_estimate=pl.CostEstimate(
            flops=0, bytes_accessed=4 * count * piece[0] * piece[1], transcendentals=0
        ),
        name="collect",
    )(to, *sources)


def precondition_kernel(chunks, left_ref, right_ref, *refs):
    grads, outs = refs[:chunks], refs[chunks : 2 * chunks]
    block, product = refs[2 * chunks :]
    size = block.shape[0]
    for c in range(chunks):
        piece = grads[c].shape[2]
        for d in range(grads[c].shape[0]):
            start = (d * chunks + c) * piece
            block[start : start + piece, :] = grads[c][d, 0]
    grad_sum = jnp.zeros((1, size), jnp.float32)
    prod_sum = jnp.zeros((1, size), jnp.float32)
    for i in range(size // STRIP):
        rows = slice(i * STRIP, (i + 1) * STRIP)
        left_part = jnp.dot(
            left_ref[0, rows, :], block[...], preferred_element_type=jnp.float32
        ).astype(jnp.bfloat16)
        strip = jnp.dot(left_part, right_ref[0], preferred_element_type=jnp.float32)
        product[rows, :] = strip
        prod_sum += jnp.sum(strip * strip, axis=0, keepdims=True)
        grad = block[rows, :].astype(jnp.float32)
        grad_sum += jnp.sum(grad * grad, axis=0, keepdims=True)
    scale = 1.0 / (size * size)
    grad_norm = jnp.sqrt(jnp.sum(grad_sum, axis=1, keepdims=True) * scale)
    prod_norm = jnp.sqrt(jnp.sum(prod_sum, axis=1, keepdims=True) * scale + 1e-06)
    ratio = grad_norm / prod_norm
    for c in range(chunks):
        piece = outs[c].shape[2]
        for d in range(outs[c].shape[0]):
            start = (d * chunks + c) * piece
            outs[c][d, 0] = (product[start : start + piece, :] * ratio).astype(jnp.bfloat16)


def precondition(left_root, right_root, pieces):
    slots, size, _ = left_root.shape
    chunks = len(pieces)
    root_spec = pl.BlockSpec((1, size, size), lambda s: (s, 0, 0))
    part = pieces[0].shape
    part_spec = pl.BlockSpec((part[0], 1) + part[2:], lambda s: (0, s, 0, 0))
    return pl.pallas_call(
        functools.partial(precondition_kernel, chunks),
        grid=(slots,),
        out_shape=[jax.ShapeDtypeStruct(part, jnp.bfloat16)] * chunks,
        in_specs=[root_spec, root_spec] + [part_spec] * chunks,
        out_specs=[part_spec] * chunks,
        scratch_shapes=[
            pltpu.VMEM((size, size), jnp.bfloat16),
            pltpu.VMEM((size, size), jnp.float32),
        ],
        compiler_params=pltpu.CompilerParams(vmem_limit_bytes=VMEM_LIMIT),
        cost_estimate=pl.CostEstimate(
            flops=4 * slots * size**3, bytes_accessed=8 * slots * size * size, transcendentals=0
        ),
        name="precondition",
    )(left_root, right_root, *pieces)


def update_kernel(parts, from_ref, to_ref, momentum_ref, *refs):
    out, buffer, loads = refs[parts * CHUNKS :]
    rows = out.shape[1] // CHUNKS
    own = from_ref.shape[0]
    copies = []
    for c in range(CHUNKS):
        near, far = refs[c * parts : c * parts + 2], refs[c * parts + 2 : (c + 1) * parts]
        pieces = []
        for i in range(own):
            for valid, piece in choose(from_ref[i], near, 0, rows):
                pieces.append((valid, piece, i))
        for k, piece in enumerate([ref.at[i] for ref in far for i in range(ref.shape[0])]):
            pieces.append((True, piece, own + k))
        for n, (valid, piece, i) in enumerate(pieces):
            to = to_ref[i]
            target = buffer.at[at_least_zero(to), pl.ds(c * rows, rows)]
            copies.append((valid & (to >= 0), piece, target, loads.at[c, n]))

    for valid, piece, target, sem in copies:

        @pl.when(valid)
        def _(piece=piece, target=target, sem=sem):
            pltpu.make_async_copy(piece, target, sem).start()

    for valid, piece, target, sem in copies:

        @pl.when(valid)
        def _(piece=piece, target=target, sem=sem):
            pltpu.make_async_copy(piece, target, sem).wait()

    for j in range(buffer.shape[0]):
        out[j] = 0.9 * momentum_ref[j] + buffer[j].astype(jnp.float32)


def update(momentum, near_from, to, chunks):
    vmem_space = pl.BlockSpec(memory_space=pltpu.VMEM)
    arrays = [x for chunk in chunks for x in chunk]
    return pl.pallas_call(
        functools.partial(update_kernel, len(chunks[0])),
        out_shape=jax.ShapeDtypeStruct(momentum.shape, jnp.float32),
        in_specs=[pl.BlockSpec(memory_space=pltpu.SMEM)] * 2
        + [vmem_space]
        + [pl.BlockSpec(memory_space=pl.ANY)] * len(arrays),
        out_specs=vmem_space,
        scratch_shapes=[
            pltpu.VMEM(momentum.shape, arrays[0].dtype),
            pltpu.SemaphoreType.DMA((CHUNKS, to.shape[0] + near_from.shape[0])),
        ],
        compiler_params=pltpu.CompilerParams(vmem_limit_bytes=VMEM_LIMIT),
        name="update",
    )(near_from, to, momentum, *arrays)


def table(match, values):
    return jnp.sum(jnp.where(match, values + 1, 0), axis=-1).astype(jnp.int32) - 1


def exchange(pieces, count):
    shape = pieces.shape
    pieces = pieces.reshape(count, -1, shape[-1])
    pieces = lax.all_to_all(pieces, "dp", split_axis=0, concat_axis=0, tiled=True)
    return pieces.reshape(shape)


def swap(piece, distance):
    groups = lax.axis_size("group")
    return lax.ppermute(piece, "group", [(g, g ^ distance) for g in range(groups)])


def shards(grad_partial, left_root, right_root, block_owner, momentum):
    dp_count = lax.axis_size("dp")
    groups = lax.axis_size("group")
    group_index = lax.axis_index("group")
    slot_count = left_root.shape[0]
    local_count, row_count, col_count = momentum.shape
    block_total = block_owner.shape[0]
    rows = lax.psum_scatter(grad_partial, "dp", scatter_dimension=2, tiled=True)[0]

    block_ids = jnp.arange(block_total, dtype=jnp.int32)
    owner_device = block_owner // slot_count
    owner_group = owner_device % groups
    owner_place = owner_device // groups * slot_count + block_owner % slot_count
    source_group = block_ids // local_count
    owner_chip = owner_group // 2
    chips = groups // 2
    earlier = (
        (block_ids[None, :] < block_ids[:, None])
        & (source_group[None, :] == source_group[:, None])
        & (owner_chip[None, :] == owner_chip[:, None])
    )
    rank_in = jnp.sum(earlier.astype(jnp.int32), axis=1)
    places = dp_count * slot_count
    offsets = 2 * jnp.arange(chips, dtype=jnp.int32)[:, None, None]
    ranked = rank_in[None, None, :] == jnp.arange(CAP, dtype=jnp.int32)[None, :, None]
    owned = (owner_group == group_index)[None, None, :]
    source = source_group[None, None, :]
    mine = table(
        (source == group_index)
        & (owner_chip[None, None, :] == (group_index ^ offsets) // 2)
        & ranked,
        block_ids - group_index * local_count,
    )
    same_to = table((source == group_index ^ offsets) & owned & ranked, owner_place)
    other_to = table((source == group_index ^ offsets ^ 1) & owned & ranked, owner_place)
    numbers = jnp.arange(local_count, dtype=jnp.int32)[:, None]
    own_to, near_to = [
        table((block_ids[None, :] == g * local_count + numbers) & owned[0], owner_place)
        for g in (group_index, group_index ^ 1)
    ]
    to_place = jnp.concatenate(
        [own_to, near_to, same_to[1:].reshape(-1), other_to[1:].reshape(-1)]
    )
    back_from = table(
        (source == group_index ^ offsets)
        & (owner_chip[None, None, :] == group_index // 2)
        & ranked,
        owner_place + jnp.where(owner_group == group_index, 0, places),
    )

    piece = row_count // CHUNKS
    sizes = [CAP] * (chips - 1)
    near = swap(rows, 1)
    came = []
    after = None
    for c in range(CHUNKS):
        sent = spread([rows], mine[1:].reshape(-1), sizes, c * piece, piece)
        if after is not None:
            *sent, after = lax.optimization_barrier((*sent, after))
            came.append(exchange(after, dp_count))
        same = [swap(sent[q - 1], 2 * q) for q in range(1, chips)]
        other = [swap(x, 1) for x in same]
        after = collect([rows, near] + same + other, c * piece, piece, to_place, places)
    came.append(exchange(after, dp_count))
    came = [x.reshape(dp_count, slot_count, piece, col_count) for x in came]
    chunks = []
    for direction in precondition(left_root, right_root, came):
        back = exchange(direction.reshape(places, piece, col_count), dp_count)
        back = [back, swap(back, 1)]
        sent = spread(back, back_from[1:].reshape(-1), sizes, 0, piece)
        chunks.append(back + [swap(sent[q - 1], 2 * q) for q in range(1, chips)])
    return update(momentum, back_from[0], mine.reshape(-1), chunks)


def solution(mesh):
    return jax.shard_map(
        shards,
        mesh=mesh,
        in_specs=(
            P("dp", "group", None, None),
            P(("dp", "group"), None, None),
            P(("dp", "group"), None, None),
            P(),
            P("group", "dp", None),
        ),
        out_specs=P("group", "dp", None),
        check_vma=False,
    )
```

```python
import functools

import jax
import jax.numpy as jnp
from jax import lax
from jax.experimental import pallas as pl
from jax.experimental.pallas import tpu as pltpu
from jax.sharding import PartitionSpec as P

CAP = 5
CHUNKS = 1
STRIP = 256
VMEM_LIMIT = 48 * 1024 * 1024
PRODUCT_VMEM_LIMIT = 32 * 1024 * 1024


def stage(copies, buffer, loads, stores):
    def load(i):
        return pltpu.make_async_copy(copies[i][1], buffer.at[i], loads.at[i])

    def store(i):
        return pltpu.make_async_copy(buffer.at[i], copies[i][2], stores.at[i])

    for i, (valid, _, _) in enumerate(copies):

        @pl.when(valid)
        def _(i=i):
            load(i).start()

    for i, (valid, _, _) in enumerate(copies):

        @pl.when(valid)
        def _(i=i):
            load(i).wait()
            store(i).start()

    for i, (valid, _, _) in enumerate(copies):

        @pl.when(valid)
        def _(i=i):
            store(i).wait()


def at_least_zero(index):
    return jnp.maximum(index, 0)


def staging(count, shape, dtype):
    return [
        pltpu.VMEM((count,) + shape, dtype),
        pltpu.SemaphoreType.DMA((count,)),
        pltpu.SemaphoreType.DMA((count,)),
    ]


def choose(index, refs, start, rows):
    found, first = [], 0
    for ref in refs:
        count = ref.shape[0]
        here = (index >= first) & (index < first + count)
        piece = jnp.clip(index - first, 0, count - 1)
        found.append((here, ref.at[piece, pl.ds(start, rows)]))
        first += count
    return found


def spread_kernel(parts, sizes, start, index_ref, *refs):
    sources, outs = refs[:parts], refs[parts : parts + len(sizes)]
    targets = [out.at[i] for out in outs for i in range(out.shape[0])]
    copies = []
    for i, target in enumerate(targets):
        for valid, piece in choose(index_ref[i], sources, start, outs[0].shape[1]):
            copies.append((valid, piece, target))
    stage(copies, *refs[parts + len(sizes) :])


def spread(sources, index, sizes, start, rows):
    count, piece = sum(sizes), (rows, sources[0].shape[2])
    dtype = sources[0].dtype
    any_space = pl.BlockSpec(memory_space=pl.ANY)
    return pl.pallas_call(
        functools.partial(spread_kernel, len(sources), sizes, start),
        out_shape=[jax.ShapeDtypeStruct((n,) + piece, dtype) for n in sizes],
        in_specs=[pl.BlockSpec(memory_space=pltpu.SMEM)] + [any_space] * len(sources),
        out_specs=[any_space] * len(sizes),
        scratch_shapes=staging(count * len(sources), piece, dtype),
        compiler_params=pltpu.CompilerParams(vmem_limit_bytes=VMEM_LIMIT),
        cost_estimate=pl.CostEstimate(
            flops=0, bytes_accessed=4 * count * piece[0] * piece[1], transcendentals=0
        ),
        name="spread",
    )(index, *sources)


def collect_kernel(parts, start, to_ref, *refs):
    sources, out = refs[:parts], refs[parts]
    rows = out.shape[1]
    pieces = []
    for ref in sources:
        first = start if ref.shape[1] > rows else 0
        pieces += [ref.at[i, pl.ds(first, rows)] for i in range(ref.shape[0])]
    copies = []
    for i, piece in enumerate(pieces):
        to = to_ref[i]
        copies.append((to >= 0, piece, out.at[at_least_zero(to)]))
    stage(copies, *refs[parts + 1 :])


def collect(sources, start, rows, to, count):
    piece = (rows, sources[0].shape[2])
    dtype = sources[0].dtype
    any_space = pl.BlockSpec(memory_space=pl.ANY)
    return pl.pallas_call(
        functools.partial(collect_kernel, len(sources), start),
        out_shape=jax.ShapeDtypeStruct((count,) + piece, dtype),
        in_specs=[pl.BlockSpec(memory_space=pltpu.SMEM)] + [any_space] * len(sources),
        out_specs=any_space,
        scratch_shapes=staging(to.shape[0], piece, dtype),
        compiler_params=pltpu.CompilerParams(vmem_limit_bytes=VMEM_LIMIT),
        cost_estimate=pl.CostEstimate(
            flops=0, bytes_accessed=4 * count * piece[0] * piece[1], transcendentals=0
        ),
        name="collect",
    )(to, *sources)


def precondition_kernel(left_ref, right_ref, grad_ref, out_ref, block, product):
    size = block.shape[0]
    places, _, piece, _ = grad_ref.shape

    def one_slot(s, carry):
        for d in range(places):
            block[d * piece : (d + 1) * piece, :] = grad_ref[d, s]
        grad_sum = jnp.zeros((1, size), jnp.float32)
        prod_sum = jnp.zeros((1, size), jnp.float32)
        for i in range(size // STRIP):
            rows = slice(i * STRIP, (i + 1) * STRIP)
            left_part = jnp.dot(
                left_ref[s, rows, :], block[...], preferred_element_type=jnp.float32
            ).astype(jnp.bfloat16)
            strip = jnp.dot(left_part, right_ref[s], preferred_element_type=jnp.float32)
            product[rows, :] = strip
            prod_sum += jnp.sum(strip * strip, axis=0, keepdims=True)
            grad = block[rows, :].astype(jnp.float32)
            grad_sum += jnp.sum(grad * grad, axis=0, keepdims=True)
        scale = 1.0 / (size * size)
        grad_norm = jnp.sqrt(jnp.sum(grad_sum, axis=1, keepdims=True) * scale)
        prod_norm = jnp.sqrt(jnp.sum(prod_sum, axis=1, keepdims=True) * scale + 1e-06)
        ratio = grad_norm / prod_norm
        for d in range(places):
            rows = slice(d * piece, (d + 1) * piece)
            out_ref[d, s] = (product[rows, :] * ratio).astype(jnp.bfloat16)
        return carry

    lax.fori_loop(0, left_ref.shape[0], one_slot, 0)


def precondition(left_root, right_root, pieces):
    slots, size, _ = left_root.shape
    vmem_space = pl.BlockSpec(memory_space=pltpu.VMEM)
    return pl.pallas_call(
        precondition_kernel,
        out_shape=jax.ShapeDtypeStruct(pieces.shape, jnp.bfloat16),
        in_specs=[vmem_space] * 3,
        out_specs=vmem_space,
        scratch_shapes=[
            pltpu.VMEM((size, size), jnp.bfloat16),
            pltpu.VMEM((size, size), jnp.float32),
        ],
        compiler_params=pltpu.CompilerParams(vmem_limit_bytes=PRODUCT_VMEM_LIMIT),
        cost_estimate=pl.CostEstimate(
            flops=4 * slots * size**3, bytes_accessed=8 * slots * size * size, transcendentals=0
        ),
        name="precondition",
    )(left_root, right_root, pieces)


def update_kernel(parts, from_ref, to_ref, momentum_ref, *refs):
    out, buffer, loads = refs[parts * CHUNKS :]
    rows = out.shape[1] // CHUNKS
    own = from_ref.shape[0]
    copies = []
    for c in range(CHUNKS):
        near, far = refs[c * parts : c * parts + 2], refs[c * parts + 2 : (c + 1) * parts]
        pieces = []
        for i in range(own):
            for valid, piece in choose(from_ref[i], near, 0, rows):
                pieces.append((valid, piece, i))
        for k, piece in enumerate([ref.at[i] for ref in far for i in range(ref.shape[0])]):
            pieces.append((True, piece, own + k))
        for n, (valid, piece, i) in enumerate(pieces):
            to = to_ref[i]
            target = buffer.at[at_least_zero(to), pl.ds(c * rows, rows)]
            copies.append((valid & (to >= 0), piece, target, loads.at[c, n]))

    for valid, piece, target, sem in copies:

        @pl.when(valid)
        def _(piece=piece, target=target, sem=sem):
            pltpu.make_async_copy(piece, target, sem).start()

    for valid, piece, target, sem in copies:

        @pl.when(valid)
        def _(piece=piece, target=target, sem=sem):
            pltpu.make_async_copy(piece, target, sem).wait()

    for j in range(buffer.shape[0]):
        out[j] = 0.9 * momentum_ref[j] + buffer[j].astype(jnp.float32)


def update(momentum, near_from, to, chunks):
    vmem_space = pl.BlockSpec(memory_space=pltpu.VMEM)
    arrays = [x for chunk in chunks for x in chunk]
    return pl.pallas_call(
        functools.partial(update_kernel, len(chunks[0])),
        out_shape=jax.ShapeDtypeStruct(momentum.shape, jnp.float32),
        in_specs=[pl.BlockSpec(memory_space=pltpu.SMEM)] * 2
        + [vmem_space]
        + [pl.BlockSpec(memory_space=pl.ANY)] * len(arrays),
        out_specs=vmem_space,
        scratch_shapes=[
            pltpu.VMEM(momentum.shape, arrays[0].dtype),
            pltpu.SemaphoreType.DMA((CHUNKS, to.shape[0] + near_from.shape[0])),
        ],
        compiler_params=pltpu.CompilerParams(vmem_limit_bytes=VMEM_LIMIT),
        name="update",
    )(near_from, to, momentum, *arrays)


def table(match, values):
    return jnp.sum(jnp.where(match, values + 1, 0), axis=-1).astype(jnp.int32) - 1


def exchange(pieces, count):
    shape = pieces.shape
    pieces = pieces.reshape(count, -1, shape[-1])
    pieces = lax.all_to_all(pieces, "dp", split_axis=0, concat_axis=0, tiled=True)
    return pieces.reshape(shape)


def swap(piece, distance):
    groups = lax.axis_size("group")
    return lax.ppermute(piece, "group", [(g, g ^ distance) for g in range(groups)])


def shards(grad_partial, left_root, right_root, block_owner, momentum):
    dp_count = lax.axis_size("dp")
    groups = lax.axis_size("group")
    group_index = lax.axis_index("group")
    slot_count = left_root.shape[0]
    local_count, row_count, col_count = momentum.shape
    block_total = block_owner.shape[0]
    rows = lax.psum_scatter(grad_partial, "dp", scatter_dimension=2, tiled=True)[0]

    block_ids = jnp.arange(block_total, dtype=jnp.int32)
    owner_device = block_owner // slot_count
    owner_group = owner_device % groups
    owner_place = owner_device // groups * slot_count + block_owner % slot_count
    source_group = block_ids // local_count
    owner_chip = owner_group // 2
    chips = groups // 2
    earlier = (
        (block_ids[None, :] < block_ids[:, None])
        & (source_group[None, :] == source_group[:, None])
        & (owner_chip[None, :] == owner_chip[:, None])
    )
    rank_in = jnp.sum(earlier.astype(jnp.int32), axis=1)
    places = dp_count * slot_count
    offsets = 2 * jnp.arange(chips, dtype=jnp.int32)[:, None, None]
    ranked = rank_in[None, None, :] == jnp.arange(CAP, dtype=jnp.int32)[None, :, None]
    owned = (owner_group == group_index)[None, None, :]
    source = source_group[None, None, :]
    mine = table(
        (source == group_index)
        & (owner_chip[None, None, :] == (group_index ^ offsets) // 2)
        & ranked,
        block_ids - group_index * local_count,
    )
    same_to = table((source == group_index ^ offsets) & owned & ranked, owner_place)
    other_to = table((source == group_index ^ offsets ^ 1) & owned & ranked, owner_place)
    numbers = jnp.arange(local_count, dtype=jnp.int32)[:, None]
    own_to, near_to = [
        table((block_ids[None, :] == g * local_count + numbers) & owned[0], owner_place)
        for g in (group_index, group_index ^ 1)
    ]
    to_place = jnp.concatenate(
        [own_to, near_to, same_to[1:].reshape(-1), other_to[1:].reshape(-1)]
    )
    back_from = table(
        (source == group_index ^ offsets)
        & (owner_chip[None, None, :] == group_index // 2)
        & ranked,
        owner_place + jnp.where(owner_group == group_index, 0, places),
    )

    piece = row_count // CHUNKS
    sizes = [CAP] * (chips - 1)
    near = swap(rows, 1)
    came = []
    after = None
    for c in range(CHUNKS):
        sent = spread([rows], mine[1:].reshape(-1), sizes, c * piece, piece)
        if after is not None:
            *sent, after = lax.optimization_barrier((*sent, after))
            came.append(exchange(after, dp_count))
        same = [swap(sent[q - 1], 2 * q) for q in range(1, chips)]
        other = [swap(x, 1) for x in same]
        after = collect([rows, near] + same + other, c * piece, piece, to_place, places)
    came.append(exchange(after, dp_count))
    came = [x.reshape(dp_count, slot_count, piece, col_count) for x in came]
    chunks = []
    for direction in [precondition(left_root, right_root, came[0])]:
        back = exchange(direction.reshape(places, piece, col_count), dp_count)
        back = [back, swap(back, 1)]
        sent = spread(back, back_from[1:].reshape(-1), sizes, 0, piece)
        chunks.append(back + [swap(sent[q - 1], 2 * q) for q in range(1, chips)])
    return update(momentum, back_from[0], mine.reshape(-1), chunks)


def solution(mesh):
    return jax.shard_map(
        shards,
        mesh=mesh,
        in_specs=(
            P("dp", "group", None, None),
            P(("dp", "group"), None, None),
            P(("dp", "group"), None, None),
            P(),
            P("group", "dp", None),
        ),
        out_specs=P("group", "dp", None),
        check_vma=False,
    )
```

```python
import functools

import jax
import jax.numpy as jnp
from jax import lax
from jax.experimental import pallas as pl
from jax.experimental.pallas import tpu as pltpu
from jax.sharding import PartitionSpec as P

CAP = 5
CHUNKS = 1
STRIP = 512
VMEM_LIMIT = 48 * 1024 * 1024
PRODUCT_VMEM_LIMIT = 32 * 1024 * 1024


def stage(copies, buffer, loads, stores):
    def load(i):
        return pltpu.make_async_copy(copies[i][1], buffer.at[i], loads.at[i])

    def store(i):
        return pltpu.make_async_copy(buffer.at[i], copies[i][2], stores.at[i])

    for i, (valid, _, _) in enumerate(copies):

        @pl.when(valid)
        def _(i=i):
            load(i).start()

    for i, (valid, _, _) in enumerate(copies):

        @pl.when(valid)
        def _(i=i):
            load(i).wait()
            store(i).start()

    for i, (valid, _, _) in enumerate(copies):

        @pl.when(valid)
        def _(i=i):
            store(i).wait()


def at_least_zero(index):
    return jnp.maximum(index, 0)


def staging(count, shape, dtype):
    return [
        pltpu.VMEM((count,) + shape, dtype),
        pltpu.SemaphoreType.DMA((count,)),
        pltpu.SemaphoreType.DMA((count,)),
    ]


def choose(index, refs, start, rows):
    found, first = [], 0
    for ref in refs:
        count = ref.shape[0]
        here = (index >= first) & (index < first + count)
        piece = jnp.clip(index - first, 0, count - 1)
        found.append((here, ref.at[piece, pl.ds(start, rows)]))
        first += count
    return found


def spread_kernel(parts, sizes, start, index_ref, *refs):
    sources, outs = refs[:parts], refs[parts : parts + len(sizes)]
    targets = [out.at[i] for out in outs for i in range(out.shape[0])]
    copies = []
    for i, target in enumerate(targets):
        for valid, piece in choose(index_ref[i], sources, start, outs[0].shape[1]):
            copies.append((valid, piece, target))
    stage(copies, *refs[parts + len(sizes) :])


def spread(sources, index, sizes, start, rows):
    count, piece = sum(sizes), (rows, sources[0].shape[2])
    dtype = sources[0].dtype
    any_space = pl.BlockSpec(memory_space=pl.ANY)
    return pl.pallas_call(
        functools.partial(spread_kernel, len(sources), sizes, start),
        out_shape=[jax.ShapeDtypeStruct((n,) + piece, dtype) for n in sizes],
        in_specs=[pl.BlockSpec(memory_space=pltpu.SMEM)] + [any_space] * len(sources),
        out_specs=[any_space] * len(sizes),
        scratch_shapes=staging(count * len(sources), piece, dtype),
        compiler_params=pltpu.CompilerParams(vmem_limit_bytes=VMEM_LIMIT),
        cost_estimate=pl.CostEstimate(
            flops=0, bytes_accessed=4 * count * piece[0] * piece[1], transcendentals=0
        ),
        name="spread",
    )(index, *sources)


def collect_kernel(parts, start, to_ref, *refs):
    sources, out = refs[:parts], refs[parts]
    rows = out.shape[1]
    pieces = []
    for ref in sources:
        first = start if ref.shape[1] > rows else 0
        pieces += [ref.at[i, pl.ds(first, rows)] for i in range(ref.shape[0])]
    copies = []
    for i, piece in enumerate(pieces):
        to = to_ref[i]
        copies.append((to >= 0, piece, out.at[at_least_zero(to)]))
    stage(copies, *refs[parts + 1 :])


def collect(sources, start, rows, to, count):
    piece = (rows, sources[0].shape[2])
    dtype = sources[0].dtype
    any_space = pl.BlockSpec(memory_space=pl.ANY)
    return pl.pallas_call(
        functools.partial(collect_kernel, len(sources), start),
        out_shape=jax.ShapeDtypeStruct((count,) + piece, dtype),
        in_specs=[pl.BlockSpec(memory_space=pltpu.SMEM)] + [any_space] * len(sources),
        out_specs=any_space,
        scratch_shapes=staging(to.shape[0], piece, dtype),
        compiler_params=pltpu.CompilerParams(vmem_limit_bytes=VMEM_LIMIT),
        cost_estimate=pl.CostEstimate(
            flops=0, bytes_accessed=4 * count * piece[0] * piece[1], transcendentals=0
        ),
        name="collect",
    )(to, *sources)


def precondition_kernel(left_ref, right_ref, grad_ref, out_ref, block, product):
    size = block.shape[0]
    places, _, piece, _ = grad_ref.shape

    def one_slot(s, carry):
        for d in range(places):
            block[d * piece : (d + 1) * piece, :] = grad_ref[d, s]
        grad_sum = jnp.zeros((1, size), jnp.float32)
        prod_sum = jnp.zeros((1, size), jnp.float32)
        for i in range(size // STRIP):
            rows = slice(i * STRIP, (i + 1) * STRIP)
            left_part = jnp.dot(
                left_ref[s, rows, :], block[...], preferred_element_type=jnp.float32
            ).astype(jnp.bfloat16)
            strip = jnp.dot(left_part, right_ref[s], preferred_element_type=jnp.float32)
            product[rows, :] = strip
            prod_sum += jnp.sum(strip * strip, axis=0, keepdims=True)
            grad = block[rows, :].astype(jnp.float32)
            grad_sum += jnp.sum(grad * grad, axis=0, keepdims=True)
        scale = 1.0 / (size * size)
        grad_norm = jnp.sqrt(jnp.sum(grad_sum, axis=1, keepdims=True) * scale)
        prod_norm = jnp.sqrt(jnp.sum(prod_sum, axis=1, keepdims=True) * scale + 1e-06)
        ratio = grad_norm / prod_norm
        for d in range(places):
            rows = slice(d * piece, (d + 1) * piece)
            out_ref[d, s] = (product[rows, :] * ratio).astype(jnp.bfloat16)
        return carry

    lax.fori_loop(0, left_ref.shape[0], one_slot, 0)


def precondition(left_root, right_root, pieces):
    slots, size, _ = left_root.shape
    vmem_space = pl.BlockSpec(memory_space=pltpu.VMEM)
    return pl.pallas_call(
        precondition_kernel,
        out_shape=jax.ShapeDtypeStruct(pieces.shape, jnp.bfloat16),
        in_specs=[vmem_space] * 3,
        out_specs=vmem_space,
        scratch_shapes=[
            pltpu.VMEM((size, size), jnp.bfloat16),
            pltpu.VMEM((size, size), jnp.float32),
        ],
        compiler_params=pltpu.CompilerParams(vmem_limit_bytes=PRODUCT_VMEM_LIMIT),
        cost_estimate=pl.CostEstimate(
            flops=4 * slots * size**3, bytes_accessed=8 * slots * size * size, transcendentals=0
        ),
        name="precondition",
    )(left_root, right_root, pieces)


def update_kernel(parts, from_ref, to_ref, momentum_ref, *refs):
    out, buffer, loads = refs[parts * CHUNKS :]
    rows = out.shape[1] // CHUNKS
    own = from_ref.shape[0]
    copies = []
    for c in range(CHUNKS):
        near, far = refs[c * parts : c * parts + 2], refs[c * parts + 2 : (c + 1) * parts]
        pieces = []
        for i in range(own):
            for valid, piece in choose(from_ref[i], near, 0, rows):
                pieces.append((valid, piece, i))
        for k, piece in enumerate([ref.at[i] for ref in far for i in range(ref.shape[0])]):
            pieces.append((True, piece, own + k))
        for n, (valid, piece, i) in enumerate(pieces):
            to = to_ref[i]
            target = buffer.at[at_least_zero(to), pl.ds(c * rows, rows)]
            copies.append((valid & (to >= 0), piece, target, loads.at[c, n]))

    for valid, piece, target, sem in copies:

        @pl.when(valid)
        def _(piece=piece, target=target, sem=sem):
            pltpu.make_async_copy(piece, target, sem).start()

    for valid, piece, target, sem in copies:

        @pl.when(valid)
        def _(piece=piece, target=target, sem=sem):
            pltpu.make_async_copy(piece, target, sem).wait()

    for j in range(buffer.shape[0]):
        out[j] = 0.9 * momentum_ref[j] + buffer[j].astype(jnp.float32)


def update(momentum, near_from, to, chunks):
    vmem_space = pl.BlockSpec(memory_space=pltpu.VMEM)
    arrays = [x for chunk in chunks for x in chunk]
    return pl.pallas_call(
        functools.partial(update_kernel, len(chunks[0])),
        out_shape=jax.ShapeDtypeStruct(momentum.shape, jnp.float32),
        in_specs=[pl.BlockSpec(memory_space=pltpu.SMEM)] * 2
        + [vmem_space]
        + [pl.BlockSpec(memory_space=pl.ANY)] * len(arrays),
        out_specs=vmem_space,
        scratch_shapes=[
            pltpu.VMEM(momentum.shape, arrays[0].dtype),
            pltpu.SemaphoreType.DMA((CHUNKS, to.shape[0] + near_from.shape[0])),
        ],
        compiler_params=pltpu.CompilerParams(vmem_limit_bytes=VMEM_LIMIT),
        name="update",
    )(near_from, to, momentum, *arrays)


def table(match, values):
    return jnp.sum(jnp.where(match, values + 1, 0), axis=-1).astype(jnp.int32) - 1


def exchange(pieces, count):
    shape = pieces.shape
    pieces = pieces.reshape(count, -1, shape[-1])
    pieces = lax.all_to_all(pieces, "dp", split_axis=0, concat_axis=0, tiled=True)
    return pieces.reshape(shape)


def swap(piece, distance):
    groups = lax.axis_size("group")
    return lax.ppermute(piece, "group", [(g, g ^ distance) for g in range(groups)])


def shards(grad_partial, left_root, right_root, block_owner, momentum):
    dp_count = lax.axis_size("dp")
    groups = lax.axis_size("group")
    group_index = lax.axis_index("group")
    slot_count = left_root.shape[0]
    local_count, row_count, col_count = momentum.shape
    block_total = block_owner.shape[0]
    rows = lax.psum_scatter(grad_partial, "dp", scatter_dimension=2, tiled=True)[0]

    block_ids = jnp.arange(block_total, dtype=jnp.int32)
    owner_device = block_owner // slot_count
    owner_group = owner_device % groups
    owner_place = owner_device // groups * slot_count + block_owner % slot_count
    source_group = block_ids // local_count
    owner_chip = owner_group // 2
    chips = groups // 2
    earlier = (
        (block_ids[None, :] < block_ids[:, None])
        & (source_group[None, :] == source_group[:, None])
        & (owner_chip[None, :] == owner_chip[:, None])
    )
    rank_in = jnp.sum(earlier.astype(jnp.int32), axis=1)
    places = dp_count * slot_count
    offsets = 2 * jnp.arange(chips, dtype=jnp.int32)[:, None, None]
    ranked = rank_in[None, None, :] == jnp.arange(CAP, dtype=jnp.int32)[None, :, None]
    owned = (owner_group == group_index)[None, None, :]
    source = source_group[None, None, :]
    mine = table(
        (source == group_index)
        & (owner_chip[None, None, :] == (group_index ^ offsets) // 2)
        & ranked,
        block_ids - group_index * local_count,
    )
    same_to = table((source == group_index ^ offsets) & owned & ranked, owner_place)
    other_to = table((source == group_index ^ offsets ^ 1) & owned & ranked, owner_place)
    numbers = jnp.arange(local_count, dtype=jnp.int32)[:, None]
    own_to, near_to = [
        table((block_ids[None, :] == g * local_count + numbers) & owned[0], owner_place)
        for g in (group_index, group_index ^ 1)
    ]
    to_place = jnp.concatenate(
        [own_to, near_to, same_to[1:].reshape(-1), other_to[1:].reshape(-1)]
    )
    back_from = table(
        (source == group_index ^ offsets)
        & (owner_chip[None, None, :] == group_index // 2)
        & ranked,
        owner_place + jnp.where(owner_group == group_index, 0, places),
    )

    piece = row_count // CHUNKS
    sizes = [CAP] * (chips - 1)
    near = swap(rows, 1)
    came = []
    after = None
    for c in range(CHUNKS):
        sent = spread([rows], mine[1:].reshape(-1), sizes, c * piece, piece)
        if after is not None:
            *sent, after = lax.optimization_barrier((*sent, after))
            came.append(exchange(after, dp_count))
        same = [swap(sent[q - 1], 2 * q) for q in range(1, chips)]
        other = [swap(x, 1) for x in same]
        after = collect([rows, near] + same + other, c * piece, piece, to_place, places)
    came.append(exchange(after, dp_count))
    came = [x.reshape(dp_count, slot_count, piece, col_count) for x in came]
    chunks = []
    for direction in [precondition(left_root, right_root, came[0])]:
        back = exchange(direction.reshape(places, piece, col_count), dp_count)
        back = [back, swap(back, 1)]
        sent = spread(back, back_from[1:].reshape(-1), sizes, 0, piece)
        chunks.append(back + [swap(sent[q - 1], 2 * q) for q in range(1, chips)])
    return update(momentum, back_from[0], mine.reshape(-1), chunks)


def solution(mesh):
    return jax.shard_map(
        shards,
        mesh=mesh,
        in_specs=(
            P("dp", "group", None, None),
            P(("dp", "group"), None, None),
            P(("dp", "group"), None, None),
            P(),
            P("group", "dp", None),
        ),
        out_specs=P("group", "dp", None),
        check_vma=False,
    )
```
